32 devices in a mesh: dp: 8 (over y, x, core), seq: 4 (over z).
Axes of the slice: x: 2, y: 2, z: 4, core: 2. Of those that a mesh axis runs over, the one named last changes fastest.
Arguments:
- tokens: bfloat16 [16, 1024, 768], P('dp', 'seq'), may hold values from -6 to 6
- seg_starts: int32 [16, 8], P('dp'), may hold values from 0 to 1023, as said below
- w_qkv: bfloat16 [768, 2304], replicated, may hold values from -0.21875 to 0.21875
- b_query: float32 [768], replicated, may hold values from -3 to 3
- b_value: float32 [768], replicated, may hold values from -3 to 3
- w_out: bfloat16 [768, 768], replicated, may hold values from -0.875 to 0.875
- b_out: float32 [768], replicated, may hold values from -3 to 3
- gain_one: float32 [768], replicated, may hold values from 0.5 to 1.5
- beta_one: float32 [768], replicated, may hold values from -3 to 3
- w_up: bfloat16 [768, 3072], replicated, may hold values from -0.21875 to 0.21875
- b_up: float32 [3072], replicated, may hold values from -3 to 3
- w_down: bfloat16 [3072, 768], replicated, may hold values from -0.109375 to 0.109375
- b_down: float32 [768], replicated, may hold values from -3 to 3
- gain_two: float32 [768], replicated, may hold values from 0.5 to 1.5
- beta_two: float32 [768], replicated, may hold values from -3 to 3
- cotangent: bfloat16 [16, 1024, 768], P('dp', 'seq'), may hold values from -6 to 6
Outputs:
- mixed: bfloat16 [16, 1024, 768], P('dp', 'seq')
- cls_rows: bfloat16 [16, 8, 768], P('dp', None, 'seq')
- grad_tokens: bfloat16 [16, 1024, 768], P('dp', 'seq')
- grad_w_qkv: float32 [768, 2304], replicated
- grad_b_query: float32 [768], replicated
- grad_b_value: float32 [768], replicated
- grad_w_out: float32 [768, 768], replicated
- grad_b_out: float32 [768], replicated
- grad_gain_one: float32 [768], replicated
- grad_beta_one: float32 [768], replicated
- grad_w_up: float32 [768, 3072], replicated
- grad_b_up: float32 [3072], replicated
- grad_w_down: float32 [3072, 768], replicated
- grad_b_down: float32 [768], replicated
- grad_gain_two: float32 [768], replicated
- grad_beta_two: float32 [768], replicated
The draws below stay inside these ranges and needn't reach their ends.
Inputs may be any that keep to these rules, and one draw needn't show every extreme that they name: `seg_starts`: in each row the starts rise strictly from 0; one segment of the row, never the last, which one drawn, begins before position 128 and reaches past 7 * 128; every other segment has at most 16 positions.
All inputs are finite; a program needn't handle non-finite values.
Results may differ from the reference program's by a relative error of at most 0.024.
Values may be sent and summed in bfloat16 or wider, within the bound.
No kernel may reach another device: no remote copies, remote signals or barrier semaphores. Data moves between devices by JAX's collectives and lax.ppermute only.
A program may use at most 192 MiB of HBM per device.

```python
import jax
import jax.numpy as jnp
from jax import lax

D = 768
HEADS = 12
FF = 3072
SEGS = 8
LENGTH = 1024
ROWS = 16


def draw_seg_starts(key, part):
    key = jax.random.fold_in(key, 11)
    key_lens, key_long, key_row = jax.random.split(key, 3)
    most = LENGTH // (8 * SEGS)
    lens = jax.random.randint(key_lens, (ROWS, SEGS - 1), 1, most + 1)
    chosen = jax.random.randint(key_row, (), 0, ROWS)
    row_ids = jnp.arange(ROWS, dtype=jnp.int32)[:, None]
    col_ids = jnp.arange(SEGS - 1, dtype=jnp.int32)[None, :]
    lens = jnp.where((row_ids == chosen) & (col_ids == SEGS - 2), 1, lens).astype(jnp.int32)
    longpos = jax.random.randint(key_long, (ROWS, 1), 0, SEGS - 1)
    prefix = jnp.concatenate([jnp.zeros((ROWS, 1), jnp.int32), jnp.cumsum(lens, axis=1).astype(jnp.int32)], axis=1)
    total = prefix[:, SEGS - 1:SEGS]
    index = jnp.arange(SEGS, dtype=jnp.int32)
    before = jnp.maximum(index - 1, 0)
    tail = LENGTH - total + prefix[:, before]
    starts = jnp.where(index[None, :] <= longpos, prefix, tail)
    return starts.astype(jnp.int32)


def block_scale(rng, extent, pieces, low, top_value):
    factor_of, own = 1.0, jax.random.fold_in(rng, 6)
    for position, blocks in pieces:
        heights = jnp.exp(jax.random.uniform(jax.random.fold_in(own, position), (blocks,), jnp.float32, low / len(pieces), top_value / len(pieces)))
        factor_of = factor_of * jnp.repeat(heights, extent[position] // blocks).reshape([-1 if axis == position else 1 for axis in range(len(extent))])
    return factor_of


def gaussian(rng, shape, deviation, limit, cuts=(), kind=jnp.bfloat16):
    level = block_scale(rng, shape, cuts, -0.22, 0.18) if cuts else 1.0
    values = jax.random.normal(rng, shape, jnp.float32) * deviation * level
    return jnp.minimum(jnp.maximum(values, -limit), limit).astype(kind)


def setup_inputs(seed: int = 0) -> dict:
    key_of = jax.random.split(jax.random.key(seed), 17)
    return {
        "tokens": gaussian(key_of[0], (ROWS, LENGTH, D), 1.0, 6.0, ((0, 8), (1, 4))),
        "seg_starts": draw_seg_starts(jax.random.fold_in(key_of[16], 71), 0),
        "w_qkv": gaussian(key_of[2], (D, 3 * D), D ** -0.5, 0.21875),
        "b_query": gaussian(key_of[3], (D,), 0.5, 3.0, (), jnp.float32),
        "b_value": gaussian(key_of[4], (D,), 0.5, 3.0, (), jnp.float32),
        "w_out": gaussian(key_of[5], (D, D), (D // 16) ** -0.5, 0.875),
        "b_out": gaussian(key_of[6], (D,), 0.5, 3.0, (), jnp.float32),
        "gain_one": jnp.clip(1.0 + 0.1 * jax.random.normal(key_of[7], (D,), jnp.float32), 0.5, 1.5),
        "beta_one": gaussian(key_of[8], (D,), 0.5, 3.0, (), jnp.float32),
        "w_up": gaussian(key_of[9], (D, FF), D ** -0.5, 0.21875),
        "b_up": gaussian(key_of[10], (FF,), 0.5, 3.0, (), jnp.float32),
        "w_down": gaussian(key_of[11], (FF, D), FF ** -0.5, 0.109375),
        "b_down": gaussian(key_of[12], (D,), 0.5, 3.0, (), jnp.float32),
        "gain_two": jnp.clip(1.0 + 0.1 * jax.random.normal(key_of[13], (D,), jnp.float32), 0.5, 1.5),
        "beta_two": gaussian(key_of[14], (D,), 0.5, 3.0, (), jnp.float32),
        "cotangent": gaussian(key_of[15], (ROWS, LENGTH, D), 1.0, 6.0, ((0, 8), (1, 4))),
    }


@jax.custom_vjp
def low(v):
    return lax.optimization_barrier(v.astype(jnp.bfloat16)).astype(jnp.float32)

@jax.custom_vjp
def low_back(v):
    return v

def low_keep(v):
    return (low(v), None)

def low_pass(kept, grad):
    return (grad,)

def back_keep(v):
    return (v, None)

def back_low(kept, grad):
    return (low(grad),)
low.defvjp(low_keep, low_pass)
low_back.defvjp(back_keep, back_low)

def norm_rows(h, gain, beta):
    mean = lax.optimization_barrier(jnp.mean(h, axis=-1, keepdims=True))
    cent = h - mean
    var = lax.optimization_barrier(jnp.mean(cent * cent, axis=-1, keepdims=True))
    return cent * lax.rsqrt(var + 1e-06) * gain + beta

def product(a, b):
    return jnp.einsum('rld,de->rle', a, b, precision=lax.Precision.HIGHEST)

def attend_row(args):
    query, key, value, seg = args
    width = query.shape[-1]
    head = width // HEADS
    q4 = query.reshape(LENGTH, HEADS, head)
    k4 = key.reshape(LENGTH, HEADS, head)
    v4 = value.reshape(LENGTH, HEADS, head)
    scores = jnp.einsum('qhd,khd->hqk', q4, k4, precision=lax.Precision.HIGHEST) * (1.0 / jnp.sqrt(jnp.float32(head)))
    scores = low_back(scores)
    mask = (seg[:, None] == seg[None, :])[None]
    scores = jnp.where(mask, scores, jnp.float32(-1e+30))
    high = lax.optimization_barrier(jnp.max(scores, axis=-1, keepdims=True))
    expo = jnp.where(mask, jnp.exp(scores - high), jnp.float32(0.0))
    probs = expo / lax.optimization_barrier(jnp.sum(expo, axis=-1, keepdims=True))
    out = jnp.einsum('hqk,khd->qhd', low(probs), v4, precision=lax.Precision.HIGHEST)
    return out.reshape(LENGTH, width)

def reference(tokens, seg_starts, w_qkv, b_query, b_value, w_out, b_out, gain_one, beta_one, w_up, b_up, w_down, b_down, gain_two, beta_two, cotangent):
    positions = jnp.arange(LENGTH, dtype=jnp.int32)
    seg = lax.optimization_barrier(jnp.sum((seg_starts[:, :, None] <= positions[None, None, :]).astype(jnp.int32), axis=1))
    width = tokens.shape[-1]

    def forward(x, wqkv, bq, bv, wo, bo, g1, e1, wu, bu, wd, bd, g2, e2):
        qkv = product(x, wqkv)
        query = low(low_back(qkv[..., :width] + bq))
        key = low(low_back(qkv[..., width:2 * width]))
        value = low(low_back(qkv[..., 2 * width:] + bv))
        attn = lax.map(jax.checkpoint(attend_row), (query, key, value, seg))
        attn = low(low_back(attn))
        branch = low_back(product(attn, wo) + bo)
        n1 = norm_rows(x + branch, g1, e1)
        pre = low_back(product(low(n1), wu) + bu)
        act = low(jax.nn.gelu(pre, approximate=False))
        ffn = low_back(product(act, wd) + bd)
        return norm_rows(n1 + ffn, g2, e2)
    params = (tokens.astype(jnp.float32), w_qkv.astype(jnp.float32), b_query, b_value, w_out.astype(jnp.float32), b_out, gain_one, beta_one, w_up.astype(jnp.float32), b_up, w_down.astype(jnp.float32), b_down, gain_two, beta_two)
    out, pull = jax.vjp(forward, *params)
    grads = pull(cotangent.astype(jnp.float32))
    mixed = out.astype(jnp.bfloat16)
    cls_rows = jnp.take_along_axis(mixed, seg_starts[:, :, None], axis=1)
    return (mixed, cls_rows, grads[0].astype(jnp.bfloat16), grads[1], grads[2], grads[3], grads[4], grads[5], grads[6], grads[7], grads[8], grads[9], grads[10], grads[11], grads[12], grads[13])
```

```python
from functools import partial

import jax
import jax.numpy as jnp
from jax import lax
from jax.experimental import pallas as pl
from jax.experimental.pallas import tpu as pltpu
from jax.sharding import PartitionSpec as P

HEADS = 12
LINE = ("core", "seq")
F32, BF16 = jnp.float32, jnp.bfloat16
NT = (((1,), (1,)), ((), ()))
TN = (((0,), (0,)), ((), ()))
NEGATIVE = -1e30
MIB = 1 << 20


def dot(a, b, dims=(((1,), (0,)), ((), ()))):
    return lax.dot_general(a, b, dims, preferred_element_type=F32)


def whole(shape):
    return pl.BlockSpec(shape, lambda *_: (0,) * len(shape))


def call(body, grid, in_specs, out_specs, out_shape, scratch, flops, moved, vmem, ids=None):
    params = pltpu.CompilerParams(
        dimension_semantics=("arbitrary",) * len(grid), vmem_limit_bytes=vmem * MIB
    )
    return pl.pallas_call(
        body,
        grid_spec=pltpu.PrefetchScalarGridSpec(
            num_scalar_prefetch=0 if ids is None else 1,
            grid=grid,
            in_specs=in_specs,
            out_specs=out_specs,
            scratch_shapes=scratch,
        ),
        out_shape=out_shape,
        compiler_params=params,
        cost_estimate=pl.CostEstimate(flops=flops, bytes_accessed=moved, transcendentals=0),
    )


def struct(shape, kind):
    return jax.ShapeDtypeStruct(shape, kind)


def attend_body(
    x_ref, wq_ref, wk_ref, wv_ref, bq_ref, bv_ref, qhot_ref, khot_ref,
    q_ref, k_ref, v_ref, attn_ref, lse_ref,
):
    count = q_ref.shape[0]
    x = x_ref[...]
    q = ((dot(x[:count], wq_ref[...]) + bq_ref[...]).astype(BF16).astype(F32) * 0.125).astype(BF16)
    k = dot(x, wk_ref[...]).astype(BF16)
    v = (dot(x, wv_ref[...]) + bv_ref[...]).astype(BF16)
    q_ref[...] = q
    k_ref[...] = k
    v_ref[...] = v
    lane = lax.broadcasted_iota(jnp.int32, (1, 128), 1)
    lane_q = lax.broadcasted_iota(jnp.int32, (count, 128), 1)
    lse = jnp.zeros((count, 128), F32)
    ones = jnp.ones(khot_ref.shape, BF16)
    for pair in range(2):
        part = slice(128 * pair, 128 * pair + 128)
        keys = jnp.concatenate([k[:, part], khot_ref[...]], axis=1)
        attn = jnp.zeros((count, 128), F32)
        for side in range(2):
            mine = ((lane >= 64) == (side == 1)).astype(F32).astype(BF16)
            queries = jnp.concatenate([q[:, part] * mine, qhot_ref[...]], axis=1)
            scores = dot(queries, keys, NT)
            high = jnp.max(scores, axis=1, keepdims=True)
            weights = jnp.exp(scores - high).astype(BF16)
            values = jnp.concatenate([v[:, part] * mine, ones], axis=1)
            both = dot(weights, values)
            total = both[:, 128:]
            attn = attn + both[:, :128] / total
            lse = jnp.where(lane_q == 2 * pair + side, high + jnp.log(total), lse)
        attn_ref[:, part] = attn
    lse_ref[0] = jnp.transpose(lse)[:8]


def attend(x_all, w_qkv, b_query, b_value, qhot, khot):
    keys, width = x_all.shape
    count = qhot.shape[0]
    quads = width // 256
    weight = [pl.BlockSpec((width, 256), lambda i, n=n: (0, n * quads + i)) for n in range(3)]
    column = lambda rows: pl.BlockSpec((rows, 256), lambda i: (0, i))
    return call(
        attend_body,
        (quads,),
        [whole(x_all.shape), *weight, column(1), column(1), whole(qhot.shape), whole(khot.shape)],
        [column(count), column(keys), column(keys), column(count), pl.BlockSpec((1, 8, count), lambda i: (i, 0, 0))],
        [
            struct((count, width), BF16),
            struct((keys, width), BF16),
            struct((keys, width), BF16),
            struct((count, width), F32),
            struct((quads, 8, count), F32),
        ],
        [],
        13_000_000_000,
        16_000_000,
        56,
    )(x_all, w_qkv, w_qkv, w_qkv, b_query, b_value, qhot, khot)


def centre(h):
    mean = jnp.mean(h, axis=-1, keepdims=True)
    cent = h - mean
    inv = lax.rsqrt(jnp.mean(cent * cent, axis=-1, keepdims=True) + 1e-06)
    return cent * inv, inv


def norm_back(cot, unit, inv, gain):
    g = cot * gain
    return inv * (
        g - jnp.mean(g, axis=-1, keepdims=True) - unit * jnp.mean(g * unit, axis=-1, keepdims=True)
    )


def row_sum(values):
    return jnp.sum(values, axis=0, keepdims=True)


UP_STEPS = 6
CHUNKS = 8


def forward_body(
    ids, x_ref, attn_ref, wo_ref, bo_ref, g1_ref, e1_ref, wu_ref, bu_ref, wd_ref, bd_ref, g2_ref, e2_ref, cot0_ref, cot1_ref,
    mixed0_ref, mixed1_ref, n1_ref, unit_ref, inv_ref, slope_ref, dh2_ref, dffn_ref, vec_ref, send_ref, keep_ref,
    full, sums, acts,
):
    step = pl.program_id(0)
    part = wu_ref.shape[1]

    @pl.when(step == 0)
    def _():
        branch = dot(attn_ref[...].astype(BF16), wo_ref[...]) + bo_ref[...]
        unit, inv = centre(x_ref[...].astype(F32) + branch)
        n1 = unit * g1_ref[...] + e1_ref[...]
        unit_ref[...] = unit
        inv_ref[...] = jnp.broadcast_to(inv, inv_ref.shape)
        full[...] = n1
        n1_ref[...] = n1.astype(BF16)
        sums[...] = jnp.zeros_like(sums)

    @pl.when(step < UP_STEPS)
    def _():
        pre = dot(n1_ref[...], wu_ref[...]) + bu_ref[...]
        phi = 0.5 * (1.0 + lax.erf(pre * 0.7071067811865476))
        slope = phi + pre * (jnp.exp(-0.5 * pre * pre) * 0.3989422804014327)
        slope_ref[...] = slope.astype(BF16)
        act = (pre * phi).astype(BF16)
        acts[:, pl.ds(pl.multiple_of(step * part, part), part)] = act
        sums[...] += dot(act, wd_ref[...])

    @pl.when(step == UP_STEPS - 1)
    def _():
        h2 = full[...] + sums[...] + bd_ref[...]
        unit, inv = centre(h2)
        cot = jnp.concatenate([cot0_ref[...], cot1_ref[...]], axis=0).astype(F32)
        mixed = (unit * g2_ref[...] + e2_ref[...]).astype(BF16)
        half = mixed0_ref.shape[0]
        mixed0_ref[...] = mixed[:half]
        mixed1_ref[...] = mixed[half:]
        dh2 = norm_back(cot, unit, inv, g2_ref[...])
        dh2_ref[...] = dh2
        dffn = dh2.astype(BF16)
        dffn_ref[...] = dffn
        vec_ref[...] = jnp.concatenate(
            [
                row_sum(cot * unit),
                row_sum(cot),
                row_sum(dffn.astype(F32)),
                jnp.zeros((5, cot.shape[1]), F32),
            ],
            axis=0,
        )

    @pl.when(step >= UP_STEPS)
    def _():
        chunk = ((step - UP_STEPS) ^ 4) ^ (ids[0] >> 2)
        grad = dot(acts[:, pl.ds(pl.multiple_of(chunk * 384, 384), 384)], dffn_ref[...], TN)
        grad = grad.astype(BF16)
        rows = grad.shape[0] // 4

        @pl.when(step < UP_STEPS + 4)
        def _():
            for i in range(4):
                send_ref[(ids[0] & 3) ^ i] = grad[i * rows : (i + 1) * rows]

        @pl.when(step >= UP_STEPS + 4)
        def _():
            for i in range(4):
                keep_ref[(ids[0] & 3) ^ i] = grad[i * rows : (i + 1) * rows]


def forward(ids, x_all, attn, w_out, b_out, g1, e1, w_up, b_up, w_down, b_down, g2, e2, cot):
    count, width = attn.shape
    half = (count // 2, width)
    hidden = w_up.shape[1]
    part = hidden // UP_STEPS
    up = lambda s, *_: (0, jnp.minimum(s, UP_STEPS - 1))
    down = lambda s, *_: (jnp.minimum(s, UP_STEPS - 1), 0)
    line = whole((1, width))
    block = (4, hidden // 32, width)
    return call(
        forward_body,
        (UP_STEPS + CHUNKS,),
        [
            whole((count, width)), whole((count, width)), whole((width, width)), line, line, line,
            pl.BlockSpec((width, part), up), pl.BlockSpec((1, part), up), pl.BlockSpec((part, width), down),
            line, line, line, whole(half), whole(half),
        ],
        [
            whole(half), whole(half), whole((count, width)), whole((count, width)), whole((count, 128)),
            pl.BlockSpec((count, part), up), whole((count, width)), whole((count, width)), whole((8, width)),
            pl.BlockSpec(block, lambda s, *_: (jnp.clip(s - UP_STEPS, 0, 3), 0, 0)),
            pl.BlockSpec(block, lambda s, *_: (jnp.clip(s - UP_STEPS - 4, 0, 3), 0, 0)),
        ],
        [
            struct(half, BF16), struct(half, BF16), struct((count, width), BF16), struct((count, width), F32),
            struct((count, 128), F32), struct((count, hidden), BF16), struct((count, width), F32),
            struct((count, width), BF16), struct((8, width), F32),
            struct((16, hidden // 32, width), BF16), struct((16, hidden // 32, width), BF16),
        ],
        [pltpu.VMEM((count, width), F32), pltpu.VMEM((count, width), F32), pltpu.VMEM((count, hidden), BF16)],
        8_000_000_000,
        30_000_000,
        56,
        ids,
    )(ids, x_all, attn, w_out, b_out, g1, e1, w_up, b_up, w_down, b_down, g2, e2, *cot)


def back_step(ids, dffn_ref, wd_ref, wu_ref, slope_ref, n1_ref, out_ref, bu_ref, sums):
    dact = dot(dffn_ref[...], wd_ref[...], NT)
    dpre = (dact * slope_ref[...].astype(F32)).astype(BF16)
    bu_ref[...] = jnp.broadcast_to(row_sum(dpre.astype(F32))[None], bu_ref.shape)
    sums[...] += dot(dpre, wu_ref[...], NT)
    grad = dot(n1_ref[...], dpre, TN).astype(BF16)
    rows, part = out_ref.shape[1], dpre.shape[1]
    for i in range(4):
        block = (ids[1] & 3) ^ i
        at = 2 * i * rows
        out_ref[block, :, :part] = grad[at : at + rows]
        out_ref[block, :, part:] = grad[at + rows : at + 2 * rows]


def back_send_body(ids, dffn_ref, wd_ref, wu_ref, slope_ref, n1_ref, dh2_ref, out_ref, bu_ref, sum_ref):
    step = pl.program_id(0)

    @pl.when(step == 0)
    def _():
        sum_ref[...] = dh2_ref[...]

    back_step(ids, dffn_ref, wd_ref, wu_ref, slope_ref, n1_ref, out_ref, bu_ref, sum_ref)


def place_rows(ids, which, grads, send_ref, keep_ref):
    rows, part = keep_ref.shape[1:]
    core, mine = ids[0] >> 4, ids[which] & 15
    for side, ref in ((core, keep_ref), (1 - core, send_ref)):
        at = pl.multiple_of(side * part, 128)

        def place(j, carry, at=at, ref=ref):
            from_row = pl.multiple_of((j ^ mine) * rows, 16)
            ref[j] = grads[pl.ds(from_row, rows), pl.ds(at, part)]
            return carry

        lax.fori_loop(0, 16, place, 0)


def back_keep_body(
    ids, dffn_ref, wd_ref, wu_ref, slope_ref, n1_ref, part_ref, unit_ref, inv_ref, g1_ref, attn_ref, wo_ref,
    out_ref, bu_ref, dh1_ref, dattn_ref, osend_ref, okeep_ref, vec_ref,
    sums, grads,
):
    step = pl.program_id(0)

    @pl.when(step == 0)
    def _():
        sums[...] = part_ref[...]

    back_step(ids, dffn_ref, wd_ref, wu_ref, slope_ref, n1_ref, out_ref, bu_ref, sums)

    @pl.when(step == 3)
    def _():
        dn1 = sums[...]
        unit = unit_ref[...]
        dh1 = norm_back(dn1, unit, inv_ref[:, :1], g1_ref[...])
        dh1_ref[...] = dh1
        dbranch = dh1.astype(BF16)
        dattn_ref[...] = dot(dbranch, wo_ref[...], NT).astype(BF16)
        grads[...] = dot(attn_ref[...].astype(BF16), dbranch, TN).astype(BF16)
        place_rows(ids, 0, grads, osend_ref, okeep_ref)
        vec_ref[...] = jnp.concatenate(
            [
                row_sum(dn1 * unit),
                row_sum(dn1),
                row_sum(dbranch.astype(F32)),
                jnp.zeros((5, dn1.shape[1]), F32),
            ],
            axis=0,
        )


def back(first, ids, dffn, w_down, w_up, slope, n1, *more):
    count, width = dffn.shape
    hidden = w_up.shape[1]
    part = hidden // CHUNKS
    true = lambda s, ids: s ^ first ^ (ids[1] >> 2)
    piece = (16, width // 8, 2 * part)
    full = whole((count, width))
    in_specs = [
        full,
        pl.BlockSpec((part, width), lambda s, ids: (true(s, ids), 0)),
        pl.BlockSpec((width, part), lambda s, ids: (0, true(s, ids))),
        pl.BlockSpec((count, part), lambda s, ids: (0, true(s, ids))),
        full, full,
    ]
    out_specs = [pl.BlockSpec((4, *piece[1:]), lambda s, ids: (s, 0, 0)), pl.BlockSpec((1, 8, part), lambda s, ids: ((true(s, ids)) & 3, 0, 0))]
    out_shape = [struct(piece, BF16), struct((4, 8, part), F32)]
    if first:
        out_specs += [full]
        out_shape += [struct((count, width), F32)]
        body, scratch = back_send_body, []
    else:
        in_specs += [full, whole((count, 128)), whole((1, width)), full, whole((width, width))]
        small = (16, width // 16, width // 2)
        out_specs += [full, full, whole(small), whole(small), whole((8, width))]
        out_shape += [
            struct((count, width), F32), struct((count, width), BF16), struct(small, BF16), struct(small, BF16),
            struct((8, width), F32),
        ]
        body, scratch = back_keep_body, [pltpu.VMEM((count, width), F32), pltpu.VMEM((width, width), BF16)]
    return call(
        body, (4,), in_specs, out_specs, out_shape, scratch, 5_000_000_000, 16_000_000, 56, ids
    )(ids, dffn, w_down, w_up, slope, n1, *more)


def attend_back_body(
    quad, ids, x_ref, q_ref, k_ref, v_ref, dattn_ref, attn_ref, lse_ref, qhot_ref, khot_ref,
    send_ref, keep_ref, dq_ref, dk_ref, dv_ref, vec_ref,
    grads, dqs, dks, dvs,
):
    count = q_ref.shape[0]
    lane = lax.broadcasted_iota(jnp.int32, (1, 128), 1)

    dqs[...] = jnp.zeros_like(dqs)
    dks[...] = jnp.zeros_like(dks)
    dvs[...] = jnp.zeros_like(dvs)

    def one_head(head, carry):
        part = pl.ds(pl.multiple_of((head >> 1) * 128, 128), 128)
        mine = ((lane >> 6) == (head & 1)).astype(F32)
        k, do = k_ref[:, part], dattn_ref[:, part]
        delta = row_sum(jnp.transpose(do.astype(F32) * attn_ref[:, part] * mine))
        mine = mine.astype(BF16)
        queries = q_ref[:, part] * mine
        douts = do * mine
        keys = jnp.concatenate([k, khot_ref[...]], axis=1)
        scores = dot(keys, jnp.concatenate([queries, qhot_ref[...]], axis=1), NT)
        probs = jnp.exp(scores - lse_ref[0, pl.ds(head, 1)])
        dprobs = dot(v_ref[:, part], douts, NT)
        dscores = (probs * (dprobs - delta)).astype(BF16)
        dvs[:, part] += dot(probs.astype(BF16), douts)
        dks[:, part] += dot(dscores, queries)
        dqs[:, part] += dot(dscores, k * mine, TN)
        return carry

    lax.fori_loop(0, 4, one_head, 0)
    dq = (dqs[...] * 0.125).astype(BF16)
    dk = dks[...].astype(BF16)
    dv = dvs[...].astype(BF16)
    vec_ref[...] = jnp.concatenate(
        [row_sum(dq.astype(F32)), row_sum(dv.astype(F32)), jnp.zeros((6, 256), F32)], axis=0
    )
    x = x_ref[...]
    for n, (left, right) in enumerate(((x[:count], dq), (x, dk), (x, dv))):
        grads[:, 256 * n : 256 * n + 256] = dot(left, right, TN).astype(BF16)
    dq_ref[...] = dq
    dk_ref[...] = dk
    dv_ref[...] = dv
    place_rows(ids, 1 if quad else 0, grads, send_ref, keep_ref)


def attend_back(quad, ids, x_all, q, k, v, dattn, attn, lse, qhot, khot):
    keys, width = x_all.shape
    count = q.shape[0]
    column = lambda rows: pl.BlockSpec((rows, 256), lambda i, ids: (0, quad))
    piece = (16, width // 16, width // 2)
    return call(
        partial(attend_back_body, quad),
        (1,),
        [
            whole(x_all.shape), column(count), column(keys), column(keys), column(count), column(count),
            pl.BlockSpec((1, 8, count), lambda i, ids: (quad, 0, 0)), whole(qhot.shape), whole(khot.shape),
        ],
        [whole(piece)] * 2 + [whole((count, 256)), whole((keys, 256)), whole((keys, 256)), whole((8, 256))],
        [struct(piece, BF16)] * 2
        + [
            struct((count, 256), BF16), struct((keys, 256), BF16), struct((keys, 256), BF16),
            struct((8, 256), F32),
        ],
        [
            pltpu.VMEM((width, width), BF16), pltpu.VMEM((count, 256), F32),
            pltpu.VMEM((keys, 256), F32), pltpu.VMEM((keys, 256), F32),
        ],
        12_000_000_000,
        10_000_000,
        58,
        ids,
    )(ids, x_all, q, k, v, dattn, attn, lse, qhot, khot)


def tokens_back_body(*refs):
    dqs, dks, dvs = refs[:3], refs[3:6], refs[6:9]
    w_ref, dh1_ref, own_ref, there_ref = refs[9:]
    count, width = dh1_ref.shape
    own, there = dh1_ref[...], None
    for quad in range(3):
        wq, wk, wv = (w_ref[:, n * width + 256 * quad : n * width + 256 * quad + 256] for n in range(3))
        dk, dv = dks[quad][...], dvs[quad][...]
        own = own + (dot(dqs[quad][...], wq, NT) + dot(dk[:count], wk, NT) + dot(dv[:count], wv, NT))
        rest = dot(dk[count:], wk, NT) + dot(dv[count:], wv, NT)
        there = rest if there is None else there + rest
    own_ref[...] = own
    there_ref[...] = there.astype(BF16)


def tokens_back(dqs, dks, dvs, w_qkv, dh1):
    operands = (*dqs, *dks, *dvs, w_qkv, dh1)
    return call(
        tokens_back_body,
        (1,),
        [whole(a.shape) for a in operands],
        [whole(dh1.shape)] * 2,
        [struct(dh1.shape, F32), struct(dh1.shape, BF16)],
        [],
        6_000_000_000,
        12_000_000,
        56,
    )(*operands)


def unfold_down_body(ids, own_ref, other_ref, out_ref):
    step = pl.program_id(0)
    rows = own_ref.shape[1]
    for half, ref in enumerate((own_ref, other_ref)):

        @pl.when(step // 4 == half)
        def _(ref=ref):
            for i in range(4):
                out_ref[i * rows : (i + 1) * rows] = ref[(ids[0] & 3) ^ i].astype(F32)


def unfold_down(ids, own, other, shape):
    _, rows, columns = own.shape
    block = (4, rows, columns)
    return call(
        unfold_down_body,
        (CHUNKS,),
        [
            pl.BlockSpec(block, lambda s, ids: (jnp.minimum(s, 3), 0, 0)),
            pl.BlockSpec(block, lambda s, ids: (jnp.maximum(s - 4, 0), 0, 0)),
        ],
        pl.BlockSpec((4 * rows, columns), lambda s, ids: (s ^ (ids[0] >> 2), 0)),
        struct(shape, F32),
        [],
        0,
        16_000_000,
        32,
        ids,
    )(ids, own, other)


def unfold_up_body(ids, own_ref, other_ref, out_ref):
    step = pl.program_id(0)
    rows, part = own_ref.shape[1], out_ref.shape[1]
    for half, ref in enumerate((own_ref, other_ref)):

        @pl.when(step // 4 == half)
        def _(ref=ref):
            for i in range(4):
                at = 2 * i * rows
                block = ref[(ids[1] & 3) ^ i].astype(F32)
                out_ref[at : at + rows] = block[:, :part]
                out_ref[at + rows : at + 2 * rows] = block[:, part:]


def unfold_up(ids, own, other, shape):
    _, rows, columns = own.shape
    block = (4, rows, columns)
    return call(
        unfold_up_body,
        (CHUNKS,),
        [
            pl.BlockSpec(block, lambda s, ids: (jnp.minimum(s, 3), 0, 0)),
            pl.BlockSpec(block, lambda s, ids: (jnp.maximum(s - 4, 0), 0, 0)),
        ],
        pl.BlockSpec((8 * rows, columns // 2), lambda s, ids: (0, s ^ (ids[1] >> 2))),
        struct(shape, F32),
        [],
        0,
        16_000_000,
        32,
        ids,
    )(ids, own, other)


def unfold_two_body(ids, a_own, a_other, b_own, b_other, qkv_ref, out_ref):
    rows = a_own.shape[1]
    for core in range(2):

        @pl.when((ids[2] >> 4) == core)
        def _(core=core):
            for i in range(4):
                at = slice(i * rows, (i + 1) * rows)
                for half, a, b in ((core, a_own, b_own), (1 - core, a_other, b_other)):
                    a = a[(ids[2] & 3) ^ i].astype(F32)
                    b = b[(ids[3] & 3) ^ i].astype(F32)
                    for quad, grad in enumerate((a[:, :384], b[:, :384], b[:, 384:])):
                        col = 256 * quad
                        if half == 0:
                            qkv_ref[at, col : col + 256] = grad[:, :256]
                            qkv_ref[at, 768 + col : 768 + col + 128] = grad[:, 256:]
                        else:
                            qkv_ref[at, 768 + col + 128 : 768 + col + 256] = grad[:, :128]
                            qkv_ref[at, 1536 + col : 1536 + col + 256] = grad[:, 128:]
                    out_ref[at, 384 * half : 384 * half + 384] = a[:, 384:]


def unfold_two(ids, a_own, a_other, b_own, b_other):
    _, rows, columns = a_own.shape
    width = 16 * rows
    block = (4, rows, columns)
    source = lambda n: pl.BlockSpec(block, lambda s, ids: (s ^ ((ids[n] >> 2) & 3), 0, 0))
    return call(
        unfold_two_body,
        (4,),
        [source(2), source(2), source(3), source(3)],
        [
            pl.BlockSpec((4 * rows, 3 * width), lambda s, ids: (s, 0)),
            pl.BlockSpec((4 * rows, width), lambda s, ids: (s, 0)),
        ],
        [struct((width, 3 * width), F32), struct((width, width), F32)],
        [],
        0,
        16_000_000,
        32,
        ids,
    )(ids, a_own, a_other, b_own, b_other)


class Moves:
    def __init__(self, pairs, seq_count):
        self.pairs, self.seq_count = pairs, seq_count
        devices = [(core, z) for core in range(2) for z in range(seq_count)]
        self.to_rows = []
        for k in range(2):
            self.to_rows.append(
                [
                    (core * seq_count + z, z // 2 * seq_count + 2 * core + (k ^ (z & 1)))
                    for core, z in devices
                ]
            )
        self.from_rows = [[(b, a) for a, b in perm] for perm in self.to_rows]
        self.rest = pairs // 4

    @staticmethod
    def swap(values, axis, count, bit):
        return lax.ppermute(values, axis, [(i, i ^ bit) for i in range(count)])

    def core(self, values):
        return self.swap(values, "core", 2, 1)

    def quad(self, values, bit):
        return self.swap(values, "quad", 4, bit)

    def line(self, values, bit):
        return self.swap(values, "seq", self.seq_count, bit)


def add(a, b):
    return (a.astype(F32) + b.astype(F32)).astype(BF16)


def sum_rest(moves, values):
    bit = 1
    while bit < moves.rest:
        values = values + moves.swap(values, "rest", moves.rest, bit)
        bit *= 2
    return values


class Clock:
    def __init__(self):
        self.mark, self.stopped = None, False

    def stop(self):
        self.stopped = True

    def tie(self, *values):
        if self.stopped or self.mark is None:
            return values
        return lax.optimization_barrier((*values, self.mark))[:-1]


def halve(clock, keep, got):
    keep, got = clock.tie(keep, got)
    half = keep.shape[0] // 2
    send = add(keep[half:], got[half:])
    clock.mark = send
    return add(keep[:half], got[:half]), send


def total(parts):
    return sum(part.astype(F32) for part in parts).astype(BF16)


def send_blocks(clock, parts, first, last):
    parts = list(clock.tie(*parts))
    send = total([part[first:last] for part in parts])
    clock.mark = send
    return parts, send


def halve_parts(clock, first, second):
    values = clock.tie(*first, *second)
    both = values[: len(first)], values[len(first) :]
    send = jnp.concatenate([total([p[2:4] for p in parts]) for parts in both], axis=1)
    clock.mark = send
    return jnp.concatenate([total([p[:2] for p in parts]) for parts in both], axis=1), send


def halve_wide(keep, got):
    half = keep[0].shape[0] // 2
    keeps, sends = zip(
        *((add(a[:half], b[:half]), add(a[half:], b[half:])) for a, b in zip(keep, got))
    )
    return jnp.concatenate(keeps, axis=2), jnp.concatenate(sends, axis=2)


def halve_both(clock, keep, got):
    *values, = clock.tie(*keep, *got)
    half = keep[0].shape[0] // 2
    sums = [add(a, b) for a, b in zip(values[:2], values[2:])]
    send = jnp.concatenate([v[half:] for v in sums], axis=1)
    clock.mark = send
    return jnp.concatenate([v[:half] for v in sums], axis=1), send


def whole_sum(clock, moves, keep, got):
    keep, got = clock.tie(keep, got)
    held = sum_rest(moves, add(keep, got))
    clock.mark = held
    return held


def join(clock, *parts):
    parts = clock.tie(*parts)
    held = jnp.concatenate(parts, axis=0)
    clock.mark = held
    return held


def split(clock, *parts):
    parts = clock.tie(*parts)
    held = jnp.concatenate(parts, axis=0)
    half = held.shape[1] // 2
    first, second = held[:, :half], held[:, half:]
    clock.mark = second
    return first, second


def on_device(
    moves,
    tokens,
    seg_starts,
    w_qkv,
    b_query,
    b_value,
    w_out,
    b_out,
    gain_one,
    beta_one,
    w_up,
    b_up,
    w_down,
    b_down,
    gain_two,
    beta_two,
    cotangent,
):
    rows, group, width = tokens.shape
    hidden = w_up.shape[1]
    quad, core, z = lax.axis_index("quad"), lax.axis_index("core"), lax.axis_index("seq")
    odd = z & 1
    x_bit, y_bit = quad & 1, quad >> 1
    z_bits = (z & 1) * 2 + (z >> 1)
    x_first = core * 16 + x_bit * 8 + y_bit * 4 + z_bits
    y_first = core * 16 + y_bit * 8 + x_bit * 4 + z_bits
    ids = jnp.stack([x_first, y_first, x_first, y_first]).astype(jnp.int32)
    line = lambda vector: vector.reshape(1, -1)

    def to_rows(values):
        return [
            lax.ppermute(jnp.where(odd == k, values[0], values[1]), LINE, moves.to_rows[k])
            for k in range(2)
        ]

    def from_rows(values):
        return [lax.ppermute(values[k], LINE, moves.from_rows[k]) for k in range(2)]

    def in_order(both):
        return jnp.where(odd == 0, jnp.stack(both), jnp.stack(both[::-1]))

    starts_here = jnp.where(odd == 0, seg_starts[0], seg_starts[1])
    starts_there = moves.core(starts_here)
    starts = jnp.where(core == z // 2, starts_here, starts_there)
    mine = to_rows(tokens)
    other = [moves.core(piece) for piece in mine]
    x_all = jnp.concatenate(mine + other, axis=0)
    count = 2 * group
    cotangent, x_all = lax.optimization_barrier((cotangent, x_all))
    cot = to_rows(cotangent)

    lane = jnp.arange(group, dtype=jnp.int32)
    positions = jnp.concatenate(
        [(2 * side + (odd ^ k)) * group + lane for side in (core, 1 - core) for k in range(2)]
    )
    seg = jnp.sum((starts[None, :] <= positions[:, None]).astype(jnp.int32), axis=1)
    same = seg[:, None] == jnp.arange(128, dtype=jnp.int32)[None, :]
    qhot = same[:count].astype(BF16)
    khot = jnp.where(same, 0.0, NEGATIVE).astype(BF16)

    q, k, v, attn, lse = attend(x_all, w_qkv, line(b_query), line(b_value), qhot, khot)
    mixed0, mixed1, n1, unit, inv, slope, dh2, dffn, vec_two, d_send, d_keep = forward(
        ids, x_all, attn, w_out, line(b_out), line(gain_one), line(beta_one), w_up, line(b_up), w_down,
        line(b_down), line(gain_two), line(beta_two), cot,
    )
    clock = Clock()
    clock.mark = dffn
    core_swap, quad_swap, line_swap = moves.core, moves.quad, moves.line
    d_got = core_swap(d_send)
    u_send, bu_there, part = back(4, ids, dffn, w_down, w_up, slope, n1, dh2)
    clock.mark = part
    u_got = core_swap(u_send)
    d_sums, d_send = send_blocks(clock, [d_keep, d_got], 8, 16)
    d_sums.append(quad_swap(d_send, 1))
    mixed = from_rows(clock.tie(mixed0, mixed1))
    (dffn,) = clock.tie(dffn)
    u_keep, bu_here, dh1, dattn, o_send, o_keep, vec_one = back(
        0, ids, dffn, w_down, w_up, slope, n1, part, unit, inv, line(gain_one), attn, w_out
    )
    clock.mark = vec_one
    u_keep, *mixed = clock.tie(u_keep, *mixed)
    u_sums, u_send = send_blocks(clock, [u_keep, u_got], 8, 16)
    u_sums.append(quad_swap(u_send, 2))
    heads = (ids, x_all, q, k, v)
    tail = (attn, lse, qhot, khot)
    (dattn,) = clock.tie(dattn)
    a_send, a_keep, *grads_a, vec_a = attend_back(0, *heads, dattn, *tail)
    clock.mark = vec_a
    a_got = core_swap(a_send)
    d_sums, d_send = send_blocks(clock, d_sums, 4, 8)
    d_sums.append(quad_swap(d_send, 2))
    (dattn,) = clock.tie(dattn)
    b_send, b_keep, *grads_b, vec_b = attend_back(1, *heads, dattn, *tail)
    clock.mark = vec_b
    b_got = core_swap(b_send)
    u_sums, u_send = send_blocks(clock, u_sums, 4, 8)
    u_sums.append(quad_swap(u_send, 1))
    (dattn,) = clock.tie(dattn)
    c_send, c_keep, *grads_c, vec_c = attend_back(2, *heads, dattn, *tail)
    clock.mark = vec_c
    c_got = core_swap(c_send)
    o_got = core_swap(clock.tie(o_send)[0])

    def close(*values):
        return lax.optimization_barrier(values)

    du_keep, du_send = halve_parts(clock, d_sums, u_sums)
    du_got = line_swap(du_send, 1)
    bu_here, bu_there, vec_one, vec_two, vec_a, vec_b, vec_c, _ = close(
        bu_here, bu_there, vec_one, vec_two, vec_a, vec_b, vec_c, du_send
    )
    bu_here, bu_there = bu_here[:, 0].reshape(1, -1), bu_there[:, 0].reshape(1, -1)
    g_bu = jnp.where(
        core == 0,
        jnp.concatenate([bu_here, bu_there], axis=1),
        jnp.concatenate([bu_there, bu_here], axis=1),
    )
    vec_zero = jnp.concatenate([vec_a, vec_b, vec_c], axis=1)
    vectors = jnp.concatenate(
        [vec_zero[:2], vec_one[:3], vec_two[:3], g_bu.reshape(-1, width)], axis=0
    )
    vec_got = core_swap(vectors)
    a_keep, a_got, b_keep, b_got, vectors, vec_got = close(
        (a_keep, o_keep), (a_got, o_got), (b_keep, c_keep), (b_got, c_got), vectors, vec_got
    )
    clock.stop()
    a_keep, a_send = halve_wide(a_keep, a_got)
    b_keep, b_send = halve_wide(b_keep, b_got)
    a_got, b_got = quad_swap(a_send, 1), quad_swap(b_send, 2)
    vectors = vectors + vec_got
    vec_got = quad_swap(vectors, 1)
    du_keep, du_got, _, _ = close(du_keep, du_got, a_send, b_send)
    du_keep, du_send = halve(clock, du_keep, du_got)
    du_got = line_swap(du_send, 2)
    dh1, _ = close(dh1, du_send)
    dx, there = tokens_back(*zip(grads_a, grads_b, grads_c), w_qkv, dh1)
    du_keep, du_got, a_keep, a_got, b_keep, b_got, there, vectors, vec_got = close(
        du_keep, du_got, a_keep, a_got, b_keep, b_got, there, vectors, vec_got
    )
    du = whole_sum(clock, moves, du_keep, du_got)
    du_got = line_swap(du, 2)
    a_keep, a_send = halve(clock, a_keep, a_got)
    a_got = quad_swap(a_send, 2)
    b_keep, b_send = halve(clock, b_keep, b_got)
    b_got = quad_swap(b_send, 1)
    there_got = core_swap(there)
    vectors = vectors + vec_got
    vec_got = quad_swap(vectors, 2)
    du, du_got, a_keep, a_got, b_keep, b_got, there_got, vectors, vec_got = close(
        du, du_got, a_keep, a_got, b_keep, b_got, there_got, vectors, vec_got
    )
    du = join(clock, du, du_got)
    du_got = line_swap(du, 1)
    dx, there_got, _ = close(dx, there_got, du)
    dx = (dx + there_got.astype(F32)).astype(BF16)
    dx = (dx[:group], dx[group:])
    pick = (starts[:, None] == positions[None, :count]).astype(BF16)
    cls = dot(pick, jnp.concatenate(close(mixed0, mixed1, du)[:2], axis=0)).astype(BF16)
    cls = cls + core_swap(cls)
    cls = jnp.swapaxes(cls.reshape(cls.shape[0], moves.seq_count, -1), 0, 1)
    ab_keep, ab_send = halve_both(clock, (a_keep, b_keep), (a_got, b_got))
    vectors = sum_rest(moves, vectors + vec_got)
    vec_got = line_swap(vectors, 1)
    du, du_got, ab_send, ab_keep, *dx, cls, vectors, vec_got = close(
        du, du_got, ab_send, ab_keep, *dx, cls, vectors, vec_got
    )
    d, u = split(clock, du, du_got)
    d_got, u_got = quad_swap(d, 2), quad_swap(u, 1)
    ab_got = line_swap(ab_send, 1)
    vectors = vectors + vec_got
    vec_got = line_swap(vectors, 2)
    cls = [
        lax.ppermute(
            lax.dynamic_index_in_dim(cls, 2 * core + (m ^ odd), 0, keepdims=False), LINE, moves.to_rows[m]
        )
        for m in range(2)
    ]
    d, d_got, u, u_got, ab_keep, ab_got, vectors, vec_got, *cls = close(
        d, d_got, u, u_got, ab_keep, ab_got, vectors, vec_got, *cls
    )
    d = join(clock, d, d_got)
    u = join(clock, u, u_got)
    d_got, u_got = quad_swap(d, 1), quad_swap(u, 2)
    ab_keep, ab_got, _, _ = close(ab_keep, ab_got, d, u)
    ab_keep, ab_send = halve(clock, ab_keep, ab_got)
    ab_got = line_swap(ab_send, 2)
    ab = whole_sum(clock, moves, ab_keep, ab_got)
    ab_got = line_swap(ab, 2)
    ab = join(clock, ab, ab_got)
    ab_got = line_swap(ab, 1)
    a, b = split(clock, ab, ab_got)
    a_got, b_got = quad_swap(a, 2), quad_swap(b, 1)
    d, d_got, u, u_got, *dx, vectors, vec_got, _, _ = close(
        d, d_got, u, u_got, *dx, vectors, vec_got, a, b
    )
    vectors = vectors + vec_got
    d = join(clock, d, d_got)
    u = join(clock, u, u_got)
    d_got, u_got = core_swap(d), core_swap(u)
    grad_tokens = from_rows(dx)
    a, a_got, b, b_got, d, u, vectors, grad_tokens[0] = close(
        a, a_got, b, b_got, d, u, vectors, grad_tokens[0]
    )
    a = join(clock, a, a_got)
    b = join(clock, b, b_got)
    a_got, b_got = quad_swap(a, 1), quad_swap(b, 2)
    d_got, u_got, _, _ = close(d_got, u_got, a, b)
    grad_w_down = unfold_down(ids, d, d_got, (hidden, width))
    grad_w_up = unfold_up(ids, u, u_got, (width, hidden))
    a, a_got, b, b_got, grad_w_down, grad_w_up, grad_tokens[1] = close(
        a, a_got, b, b_got, grad_w_down, grad_w_up, grad_tokens[1]
    )
    a = join(clock, a, a_got)
    b = join(clock, b, b_got)
    a_got, b_got = core_swap(a), core_swap(b)
    cls, grad_tokens, mixed = in_order(cls), in_order(grad_tokens), in_order(mixed)
    grad_w_qkv, grad_w_out = unfold_two(ids, a, a_got, b, b_got)
    return (
        mixed,
        cls,
        grad_tokens,
        grad_w_qkv,
        vectors[0],
        vectors[1],
        grad_w_out,
        vectors[4],
        vectors[2],
        vectors[3],
        grad_w_up,
        vectors[8:].reshape(-1),
        grad_w_down,
        vectors[7],
        vectors[5],
        vectors[6],
    )


def solution(mesh):
    pairs, seq_count = mesh.shape["dp"] // 2, mesh.shape["seq"]
    axes = ("rest", "quad", "core", "seq")
    split = jax.sharding.Mesh(mesh.devices.reshape(pairs // 4, 4, 2, seq_count), axes)
    dp = ("rest", "quad", "core")
    row = P(dp, "seq", None)
    in_specs = (row, P(dp, None)) + (P(),) * 13 + (row,)
    out_specs = (row, P(dp, None, "seq"), row) + (P(),) * 13
    return jax.shard_map(
        partial(on_device, Moves(pairs, seq_count)),
        mesh=split,
        in_specs=in_specs,
        out_specs=out_specs,
        check_vma=False,
    )
```
